32 devices in a mesh: seq: 8 (over y, x, core), head: 4 (over z).
Axes of the slice: x: 2, y: 2, z: 4, core: 2. Of those that a mesh axis runs over, the one named last changes fastest.
Arguments:
- queries: bfloat16 [2048, 64, 128], P('seq', 'head'), may hold values from -100 to 100
- key_states: bfloat16 [2048, 4, 128], P('seq'), may hold values from -6.7 to 6.7
- values: bfloat16 [2048, 4, 128], P('seq'), may hold values from -6 to 6
- grad_out: bfloat16 [2048, 64, 128], P('seq', 'head'), may hold values from -6 to 6
- picked_blocks: int32 [32, 4, 16], P('seq'), may hold values from -1 to 31, as said below
Outputs:
- grad_queries: float32 [2048, 64, 128], P('seq', 'head')
- grad_keys: float32 [2048, 4, 128], P(('seq', 'head'))
- grad_values: float32 [2048, 4, 128], P(('seq', 'head'))
The draws below stay inside these ranges and needn't reach their ends.
Inputs may be any that keep to these rules, and one draw needn't show every extreme that they name: picked_blocks[b, g, 0] = b. The query blocks come in runs of 256 / 64 (run s holds blocks s * 4 onward); for each run s and group g, the entries j >= 1 of the run's blocks that are not -1 name blocks of distinct runs, all lower than s, and there are exactly min(s, 60) of them.
All inputs are finite; a program needn't handle non-finite values.
Results may differ from the reference program's by a relative error of at most 0.02.
Values may be sent and summed in bfloat16 or wider, within the bound.
A program may use at most 64 MiB of HBM per device.

```python
import jax
import jax.numpy as jnp
from jax import lax

G = 4
HPG = 16
DQK = 128
DV = 128
BLK = 64
KSEL = 16
TOK_DEV = 256
H = 64
TOKENS = 2048
N_HEAD = 4


def attention_pair(key):
    base_key = jax.random.fold_in(key, 11)
    key_first, key_second = jax.random.split(base_key, 2)
    key_values = jnp.clip(jax.random.normal(key_first, (TOKENS, G, DQK), jnp.float32), -6.0, 6.0)
    query_values = jnp.clip(jax.random.normal(key_second, (TOKENS, G * HPG, DQK), jnp.float32), -6.0, 6.0)
    return (query_values, key_values)


def draw_queries(key, part):
    return attention_pair(key)[0].astype(jnp.bfloat16)


def draw_key_states(key, part):
    return attention_pair(key)[1].astype(jnp.bfloat16)


def draw_picked_blocks(key, part):
    per_shard = TOK_DEV // BLK
    block_total = TOKENS // BLK
    shard_total = block_total // per_shard
    slot_total = per_shard * (KSEL - 1)
    live_total = min(slot_total, shard_total)
    base_key = jax.random.fold_in(key, 23)
    order_key, within_key = jax.random.split(base_key)
    seed_keys = jax.random.split(order_key, shard_total * G)
    orders = jax.vmap(lambda single: jax.random.permutation(single, shard_total))(seed_keys)
    orders = orders.astype(jnp.int32).reshape(shard_total, G, shard_total)
    shard_ids = jnp.arange(shard_total, dtype=jnp.int32)
    earlier = shard_ids[None, None, :] < shard_ids[:, None, None]
    scores = jnp.where(earlier, orders, -1 - shard_ids[None, None, :])
    best_score, where_from = lax.top_k(scores, live_total)
    within = jax.random.randint(within_key, (shard_total, G, live_total), 0, per_shard)
    chosen = jnp.where(best_score >= 0, where_from.astype(jnp.int32) * per_shard + within, -1).astype(jnp.int32)
    padding = jnp.full((shard_total, G, slot_total - live_total), -1, jnp.int32)
    chosen = jnp.concatenate([chosen, padding], axis=2)
    chosen = chosen.reshape(shard_total, G, KSEL - 1, per_shard).transpose(0, 3, 1, 2).reshape(block_total, G, KSEL - 1)
    self_block = jnp.broadcast_to(jnp.arange(block_total, dtype=jnp.int32)[:, None, None], (block_total, G, 1))
    return jnp.concatenate([self_block, chosen], axis=2)


def level_of(rng, shape, shards, low, high):
    gain, own = 1.0, jax.random.fold_in(rng, 6)
    for dim, shards_of in shards:
        steps = jnp.exp(jax.random.uniform(jax.random.fold_in(own, dim), (shards_of,), jnp.float32, low / len(shards), high / len(shards)))
        gain = gain * jnp.repeat(steps, shape[dim] // shards_of).reshape([-1 if axis == dim else 1 for axis in range(len(shape))])
    return gain


def gaussian(own_key, dims, deviation, limit, cuts=(), kind=jnp.bfloat16):
    array = jax.random.normal(own_key, dims, jnp.float32) * deviation
    if len(cuts) > 0:
        array = level_of(own_key, dims, cuts, -0.22, 0.18) * array
    return jnp.clip(array, min=-limit, max=limit).astype(kind)


def setup_inputs(seed: int = 0) -> dict:
    splits = jax.random.split(jax.random.key(seed), 6)
    queries = draw_queries(jax.random.fold_in(splits[5], 71), 0)
    key_states = draw_key_states(jax.random.fold_in(splits[5], 71), 0)
    values = gaussian(splits[2], (TOKENS, G, DV), 1.0, 6.0, ((0, 8),))
    grad_out = gaussian(splits[3], (TOKENS, H, DV), 1.0, 6.0, ((0, 8), (1, 4)))
    picked_blocks = draw_picked_blocks(jax.random.fold_in(splits[5], 71), 0)
    return dict(queries=queries, key_states=key_states, values=values, grad_out=grad_out, picked_blocks=picked_blocks)


NEG = -1.0e30


def reference(queries, key_states, values, grad_out, picked_blocks):
    factor = DQK ** -0.5
    block_total = TOKENS // BLK
    head_dev = (G * HPG) // N_HEAD
    spans = HPG // head_dev
    key_table = key_states.reshape(block_total, BLK, G, DQK).transpose(2, 0, 1, 3)
    value_table = values.reshape(block_total, BLK, G, DV).transpose(2, 0, 1, 3)
    query_blocks = queries.reshape(block_total, BLK, G, HPG, DQK)
    grad_blocks = grad_out.reshape(block_total, BLK, G, HPG, DV)
    group_index = jnp.arange(G, dtype=jnp.int32)[:, None]
    offsets = jnp.arange(BLK, dtype=jnp.int32)
    causal = offsets[None, :] <= offsets[:, None]
    leading = jnp.arange(KSEL, dtype=jnp.int32) == 0

    def accumulate(carry, inputs):
        key_accum, value_accum = carry
        query_block, grad_block, pick_row = inputs
        live_slots = pick_row >= 0
        safe_pick = jnp.maximum(pick_row, 0).astype(jnp.int32)
        key_sets = key_table[group_index, safe_pick]
        value_sets = value_table[group_index, safe_pick]
        query_wide = query_block.astype(jnp.float32)
        grad_wide = grad_block.astype(jnp.float32)
        key_wide = key_sets.astype(jnp.float32)
        value_wide = value_sets.astype(jnp.float32)
        scores = jnp.einsum("tghd,gjkd->ghtjk", query_wide, key_wide) * factor
        visible = live_slots[:, None, None, :, None] & (jnp.logical_not(leading)[None, None, None, :, None] | causal[None, None, :, None, :])
        scores = jnp.where(visible, scores, NEG)
        maxima = jnp.max(scores, axis=(3, 4), keepdims=True)
        weights = jnp.where(visible, jnp.exp(scores - maxima), 0.0)
        attend = weights / jnp.sum(weights, axis=(3, 4), keepdims=True)
        attend_low = attend.astype(jnp.bfloat16)
        grad_prob = jnp.einsum("tghe,gjke->ghtjk", grad_wide, value_wide)
        row_dot = jnp.sum(attend * grad_prob, axis=(3, 4), keepdims=True)
        dscore = (attend * (grad_prob - row_dot)).astype(jnp.bfloat16)
        dscore_wide = dscore.astype(jnp.float32)
        grad_query = jnp.einsum("ghtjk,gjkd->tghd", dscore_wide, key_wide) * factor
        dscore_runs = dscore_wide.reshape(G, spans, head_dev, BLK, KSEL, BLK)
        attend_runs = attend_low.astype(jnp.float32).reshape(G, spans, head_dev, BLK, KSEL, BLK)
        query_runs = query_wide.reshape(BLK, G, spans, head_dev, DQK)
        grad_runs = grad_wide.reshape(BLK, G, spans, head_dev, DV)
        key_parts = jnp.einsum("gchtjk,tgchd->gcjkd", dscore_runs, query_runs) * factor
        value_parts = jnp.einsum("gchtjk,tgche->gcjke", attend_runs, grad_runs)
        key_rounded = lax.optimization_barrier(key_parts.astype(jnp.bfloat16)).astype(jnp.float32)
        value_rounded = lax.optimization_barrier(value_parts.astype(jnp.bfloat16)).astype(jnp.float32)
        key_contrib = jnp.where(leading[None, :, None, None], key_parts.sum(axis=1), key_rounded.sum(axis=1))
        value_contrib = jnp.where(leading[None, :, None, None], value_parts.sum(axis=1), value_rounded.sum(axis=1))
        target = jnp.where(live_slots, pick_row, block_total).astype(jnp.int32)
        key_accum = key_accum.at[group_index, target].add(key_contrib, mode="drop")
        value_accum = value_accum.at[group_index, target].add(value_contrib, mode="drop")
        return (key_accum, value_accum), grad_query

    start = (jnp.zeros((G, block_total, BLK, DQK), jnp.float32), jnp.zeros((G, block_total, BLK, DV), jnp.float32))
    finals, grad_query_blocks = lax.scan(accumulate, start, (query_blocks, grad_blocks, picked_blocks))
    key_accum, value_accum = finals
    grad_queries = grad_query_blocks.reshape(TOKENS, G * HPG, DQK)
    grad_keys = key_accum.transpose(1, 2, 0, 3).reshape(TOKENS, G, DQK)
    grad_values = value_accum.transpose(1, 2, 0, 3).reshape(TOKENS, G, DV)
    return (grad_queries, grad_keys, grad_values)
```

```python
import functools
import math

import jax
import jax.numpy as jnp
from jax import lax
from jax.experimental import pallas as pl
from jax.experimental.pallas import tpu as pltpu
from jax.sharding import PartitionSpec as P

G = 4
HPG = 16
BLK = 64
NEG = -1e30
MESH = pl.DeviceIdType.MESH
F32 = jnp.float32
BF16 = jnp.bfloat16
NT = (((1,), (1,)), ((), ()))


def kernel(
    shards, peers, heads_dev, chunk,
    q_hbm, go_hbm, kv_ref, wanted_ref, bias_ref,
    dq_hbm, out_ref,
    q_buf, go_buf, dq_buf, slots, key_t, bias_buf, acc, own,
    ask_out, ask_in, kv_out, ret_out, ret_in, hx_out, hx_in,
    load_sem, dq_sem, ask_ssem, ask_rsem, kv_ssem, kv_rsem,
    ret_ssem, ret_rsem, hx_ssem, hx_rsem,
):
    me = lax.axis_index("seq")
    mh = lax.axis_index("head")
    width = q_hbm.shape[1]
    factor = width ** (-0.5)
    blocks = kv_ref.shape[1] // BLK
    rows_b = q_buf.shape[0] // blocks
    part = kv_ref.shape[1] // peers
    run_total = HPG // heads_dev

    def at_block(i):
        return pl.ds(pl.multiple_of(i * BLK, BLK), BLK)

    def seq_copy(src, dst, ssem, rsem, peer):
        return pltpu.make_async_remote_copy(
            src_ref=src, dst_ref=dst, send_sem=ssem, recv_sem=rsem,
            device_id=(peer, mh), device_id_type=MESH,
        )

    def ask_copy(src_at, to, frm):
        return seq_copy(ask_out.at[src_at], ask_in.at[frm], ask_ssem.at[src_at], ask_rsem.at[frm], to)

    def kv_copy(src_at, to, frm):
        return seq_copy(
            kv_out.at[src_at], slots.at[:, at_block(frm)], kv_ssem.at[src_at], kv_rsem.at[frm], to
        )

    def ret_copy(src_at, to, frm):
        return seq_copy(ret_out.at[src_at], ret_in.at[frm], ret_ssem.at[src_at], ret_rsem.at[frm], to)

    def hx_copy(src_at, to, frm):
        return pltpu.make_async_remote_copy(
            src_ref=hx_out.at[src_at], dst_ref=hx_in.at[frm],
            send_sem=hx_ssem.at[src_at], recv_sem=hx_rsem.at[frm],
            device_id=(me, to), device_id_type=MESH,
        )

    load_q = pltpu.make_async_copy(q_hbm, q_buf, load_sem.at[0])
    load_go = pltpu.make_async_copy(go_hbm, go_buf, load_sem.at[1])
    load_q.start()
    load_go.start()

    barrier = pltpu.get_barrier_semaphore()

    @pl.loop(0, shards)
    def _(i):
        @pl.when(i != me)
        def _():
            pl.semaphore_signal(barrier, inc=1, device_id=(i, mh), device_id_type=MESH)

    @pl.loop(0, peers)
    def _(i):
        @pl.when(i != mh)
        def _():
            pl.semaphore_signal(barrier, inc=1, device_id=(me, i), device_id_type=MESH)

    @pl.loop(0, shards)
    def _(i):
        ask_out[i] = jnp.full((8, 128), wanted_ref[i], jnp.int32)

        @pl.when(i > me)
        def _():
            slots[:, at_block(i)] = jnp.zeros((2, BLK, width), BF16)

    pl.semaphore_wait(barrier, shards + peers - 2)

    @pl.loop(0, shards)
    def _(i):
        @pl.when(i < me)
        def _():
            ask_copy(i, i, me).start()

    acc[...] = jnp.zeros(acc.shape, F32)

    @pl.loop(0, shards)
    def _(i):
        @pl.when(i > me)
        def _():
            ask_copy(i, i, i).wait_recv()
            asked = ask_in[i][0:1, :]
            total = jnp.zeros((2, BLK, width), F32)
            for q in range(blocks):
                hit = (asked == q).astype(F32)
                total = total + kv_ref[:, q * BLK : (q + 1) * BLK].astype(F32) * hit[None]
            kv_out[i] = total.astype(BF16)
            kv_copy(i, i, me).start()

    load_q.wait()
    load_go.wait()

    @pl.loop(0, shards)
    def _(i):
        @pl.when(i < me)
        def _():
            kv_copy(i, i, i).wait_recv()

    scale = factor * math.log2(math.e)

    @pl.loop(0, blocks)
    def _(b):
        slots[:, at_block(me)] = kv_ref[:, at_block(b)]
        acc[:, at_block(me)] = jnp.zeros((2, BLK, width), F32)

        @pl.loop(0, shards)
        def _(i):
            bias_buf[at_block(i)] = jnp.full((BLK, chunk), bias_ref[b, i], F32)

        key_t[...] = slots[0].T

        @pl.loop(0, rows_b // chunk)
        def _(c):
            rows = pl.ds(pl.multiple_of(b * rows_b + c * chunk, chunk), chunk)
            key_row = lax.broadcasted_iota(jnp.int32, (BLK, chunk), 0)
            lane = lax.broadcasted_iota(jnp.int32, (BLK, chunk), 1)
            bias_buf[at_block(me)] = jnp.where(key_row * heads_dev <= lane + c * chunk, 0.0, NEG)
            qc = q_buf[rows]
            gc = go_buf[rows]
            s = lax.dot_general(slots[0], qc, NT, preferred_element_type=F32)
            s = s * scale + bias_buf[...]
            p = jnp.exp2(s - jnp.max(s, axis=0, keepdims=True))
            inverse = 1.0 / jnp.sum(p, axis=0, keepdims=True)
            a = p * inverse
            gp = lax.dot_general(slots[1], gc, NT, preferred_element_type=F32)
            row_dot = jnp.sum(a * gp, axis=0, keepdims=True)
            ds = (a * (gp - row_dot)).astype(BF16)
            acc[1] += jnp.dot(a.astype(BF16), gc, preferred_element_type=F32)
            acc[0] += jnp.dot(ds, qc, preferred_element_type=F32)
            dq_t = jnp.dot(key_t[...], ds, preferred_element_type=F32)
            dq_buf[rows] = (dq_t * factor).T

        own[0, at_block(b)] = acc[0, at_block(me)] * factor
        own[1, at_block(b)] = acc[1, at_block(me)]
        rows = pl.ds(pl.multiple_of(b * rows_b, rows_b), rows_b)
        pltpu.make_async_copy(dq_buf.at[rows], dq_hbm.at[rows], dq_sem.at[b]).start()

    @pl.loop(0, shards)
    def _(i):
        @pl.when(i < me)
        def _():
            ret_out[i, 0] = (acc[0, at_block(i)] * factor).astype(BF16)
            ret_out[i, 1] = acc[1, at_block(i)].astype(BF16)
            ret_copy(i, i, me).start()

    @pl.loop(0, shards)
    def _(i):
        @pl.when(i > me)
        def _():
            ret_copy(i, i, i).wait_recv()
            asked = ask_in[i][0:1, :]
            back = ret_in[i].astype(F32)
            for q in range(blocks):
                hit = (asked == q).astype(F32)
                own[:, q * BLK : (q + 1) * BLK] += back * hit[None]

    @pl.loop(0, peers)
    def _(i):
        @pl.when(i != mh)
        def _():
            hx_out[i] = own[:, pl.ds(pl.multiple_of(i * part, part), part)].astype(BF16)
            hx_copy(i, i, mh).start()

    hx_in[mh] = own[:, pl.ds(pl.multiple_of(mh * part, part), part)].astype(BF16)

    @pl.loop(0, peers)
    def _(i):
        @pl.when(i != mh)
        def _():
            hx_copy(i, i, i).wait_recv()

    for g in range(G):
        total = hx_in[g * run_total].astype(F32)
        for c in range(1, run_total):
            total = total + hx_in[g * run_total + c].astype(F32)
        out_ref[:, g] = total

    @pl.loop(0, shards)
    def _(i):
        @pl.when(i < me)
        def _():
            ask_copy(i, i, me).wait_send()
            ret_copy(i, i, me).wait_send()

        @pl.when(i > me)
        def _():
            kv_copy(i, i, me).wait_send()

    @pl.loop(0, peers)
    def _(i):
        @pl.when(i != mh)
        def _():
            hx_copy(i, i, mh).wait_send()

    @pl.loop(0, blocks)
    def _(b):
        rows = pl.ds(pl.multiple_of(b * rows_b, rows_b), rows_b)
        pltpu.make_async_copy(dq_buf.at[rows], dq_hbm.at[rows], dq_sem.at[b]).wait()


def on_device(queries, key_states, values, grad_out, picked_blocks):
    tokens_dev, heads_dev, width = queries.shape
    blocks = tokens_dev // BLK
    shards = lax.axis_size("seq")
    peers = lax.axis_size("head")
    me = lax.axis_index("seq")
    group_id = lax.axis_index("head") // (HPG // heads_dev)
    kv = jnp.stack([
        lax.dynamic_index_in_dim(key_states, group_id, 1, keepdims=False),
        lax.dynamic_index_in_dim(values, group_id, 1, keepdims=False),
    ])
    picks = lax.dynamic_index_in_dim(picked_blocks, group_id, 1, keepdims=False)[:, 1:]
    shard_ids = jnp.arange(shards, dtype=jnp.int32)
    match = (picks >= 0)[:, :, None] & ((picks // blocks)[:, :, None] == shard_ids)
    wanted = jnp.max(jnp.where(match, (picks % blocks)[:, :, None], -1), axis=(0, 1))
    bias = jnp.where(jnp.any(match, axis=1) | (shard_ids == me), 0.0, NEG).astype(F32)
    rows = tokens_dev * heads_dev
    chunk = min(256, rows // blocks)
    part = tokens_dev // peers
    keys = shards * BLK
    dma = pltpu.SemaphoreType.DMA
    any_spec = pl.BlockSpec(memory_space=pl.ANY)
    vmem = pl.BlockSpec(memory_space=pltpu.VMEM)
    smem = pl.BlockSpec(memory_space=pltpu.SMEM)
    dq, out = pl.pallas_call(
        functools.partial(kernel, shards, peers, heads_dev, chunk),
        out_shape=(
            jax.ShapeDtypeStruct((rows, width), F32),
            jax.ShapeDtypeStruct((2, G, part, width), F32),
        ),
        in_specs=[any_spec, any_spec, vmem, smem, smem],
        out_specs=(any_spec, vmem),
        scratch_shapes=[
            pltpu.VMEM((rows, width), BF16),
            pltpu.VMEM((rows, width), BF16),
            pltpu.VMEM((rows, width), F32),
            pltpu.VMEM((2, keys, width), BF16),
            pltpu.VMEM((width, keys), BF16),
            pltpu.VMEM((keys, chunk), F32),
            pltpu.VMEM((2, keys, width), F32),
            pltpu.VMEM((2, tokens_dev, width), F32),
            pltpu.VMEM((shards, 8, 128), jnp.int32),
            pltpu.VMEM((shards, 8, 128), jnp.int32),
            pltpu.VMEM((shards, 2, BLK, width), BF16),
            pltpu.VMEM((shards, 2, BLK, width), BF16),
            pltpu.VMEM((shards, 2, BLK, width), BF16),
            pltpu.VMEM((peers, 2, part, width), BF16),
            pltpu.VMEM((peers, 2, part, width), BF16),
            dma((2,)), dma((blocks,)),
            dma((shards,)), dma((shards,)), dma((shards,)), dma((shards,)),
            dma((shards,)), dma((shards,)), dma((peers,)), dma((peers,)),
        ],
        compiler_params=pltpu.CompilerParams(
            collective_id=0, has_side_effects=True, vmem_limit_bytes=48 * 1024 * 1024
        ),
    )(queries.reshape(rows, width), grad_out.reshape(rows, width), kv, wanted, bias)
    return (
        dq.reshape(tokens_dev, heads_dev, width),
        out[0].transpose(1, 0, 2),
        out[1].transpose(1, 0, 2),
    )


def solution(mesh):
    placed = (
        P("seq", "head", None),
        P("seq", None, None),
        P("seq", None, None),
        P("seq", "head", None),
        P("seq", None, None),
    )
    return jax.shard_map(
        on_device,
        mesh=mesh,
        in_specs=placed,
        out_specs=(
            P("seq", "head", None),
            P(("seq", "head"), None, None),
            P(("seq", "head"), None, None),
        ),
        check_vma=False,
    )
```

```python
import functools
import math

import jax
import jax.numpy as jnp
from jax import lax
from jax.experimental import pallas as pl
from jax.experimental.pallas import tpu as pltpu
from jax.sharding import PartitionSpec as P

G = 4
HPG = 16
BLK = 64
NEG = -1e30
MESH = pl.DeviceIdType.MESH
F32 = jnp.float32
BF16 = jnp.bfloat16
NT = (((1,), (1,)), ((), ()))


def kernel(
    shards, peers, heads_dev, chunk,
    q_hbm, go_hbm, kv_ref, wanted_ref, owner_ref, hit_ref, sel_ref,
    dq_hbm, out_ref,
    q_buf, go_buf, dq_buf, slots, key_mask, exp_buf, gp_buf, ds_buf,
    top_buf, sum_buf, dot_buf, fac_buf, mean_buf, own,
    ask_out, ask_in, kv_out, ret_out, ret_in, hx_out, hx_in,
    load_sem, dq_sem, ask_ssem, ask_rsem, kv_ssem, kv_rsem,
    ret_ssem, ret_rsem, hx_ssem, hx_rsem,
):
    me = lax.axis_index("seq")
    mh = lax.axis_index("head")
    width = q_hbm.shape[2]
    factor = width ** (-0.5)
    scale = factor * math.log2(math.e)
    blocks = kv_ref.shape[1] // BLK
    rows_b = q_buf.shape[1]
    part = kv_ref.shape[1] // peers
    run_total = HPG // heads_dev
    cuts = rows_b // chunk

    def at_block(i):
        return pl.ds(pl.multiple_of(i * BLK, BLK), BLK)

    def seq_copy(src, dst, ssem, rsem, peer):
        return pltpu.make_async_remote_copy(
            src_ref=src, dst_ref=dst, send_sem=ssem, recv_sem=rsem,
            device_id=(peer, mh), device_id_type=MESH,
        )

    def ask_copy(src_at, to, frm):
        return seq_copy(ask_out.at[src_at], ask_in.at[frm], ask_ssem.at[src_at], ask_rsem.at[frm], to)

    def kv_copy(src_at, to, frm):
        return seq_copy(
            kv_out.at[src_at], slots.at[:, at_block(frm)], kv_ssem.at[src_at], kv_rsem.at[frm], to
        )

    def ret_copy(src_at, to, frm):
        return seq_copy(ret_out.at[src_at], ret_in.at[frm], ret_ssem.at[src_at], ret_rsem.at[frm], to)

    def hx_copy(src_at, to, frm):
        return pltpu.make_async_remote_copy(
            src_ref=hx_out.at[src_at], dst_ref=hx_in.at[frm],
            send_sem=hx_ssem.at[src_at], recv_sem=hx_rsem.at[frm],
            device_id=(me, to), device_id_type=MESH,
        )

    load_q = pltpu.make_async_copy(q_hbm, q_buf, load_sem.at[0])
    load_go = pltpu.make_async_copy(go_hbm, go_buf, load_sem.at[1])
    load_q.start()
    load_go.start()

    barrier = pltpu.get_barrier_semaphore()

    @pl.loop(0, shards)
    def _(i):
        @pl.when(i != me)
        def _():
            pl.semaphore_signal(barrier, inc=1, device_id=(i, mh), device_id_type=MESH)

    @pl.loop(0, peers)
    def _(i):
        @pl.when(i != mh)
        def _():
            pl.semaphore_signal(barrier, inc=1, device_id=(me, i), device_id_type=MESH)

    @pl.loop(0, shards)
    def _(i):
        ask_out[i] = jnp.full((8, 128), wanted_ref[i], jnp.int32)

        @pl.when(i >= me)
        def _():
            ds_buf[at_block(i)] = jnp.zeros((BLK, rows_b), BF16)
            for b in range(blocks):
                key_mask[b, at_block(i)] = jnp.zeros((BLK, width), BF16)

    top_buf[...] = jnp.zeros(top_buf.shape, F32)
    sum_buf[...] = jnp.zeros(sum_buf.shape, F32)
    dot_buf[...] = jnp.zeros(dot_buf.shape, F32)

    pl.semaphore_wait(barrier, shards + peers - 2)

    @pl.loop(0, shards)
    def _(i):
        @pl.when(i < me)
        def _():
            ask_copy(i, i, me).start()

    def first_half(pair, block, keys, vals, causal):
        for c in range(cuts):
            lanes = slice(c * chunk, (c + 1) * chunk)
            rows = slice(c * chunk, (c + 1) * chunk)
            s = lax.dot_general(keys, q_buf[block, rows], NT, preferred_element_type=F32) * scale
            if causal:
                key_row = lax.broadcasted_iota(jnp.int32, (BLK, chunk), 0)
                lane = lax.broadcasted_iota(jnp.int32, (BLK, chunk), 1)
                s = jnp.where(key_row * heads_dev <= lane + c * chunk, s, NEG)
            gp = lax.dot_general(vals, go_buf[block, rows], NT, preferred_element_type=F32)
            top = jnp.max(s, axis=0, keepdims=True)
            e = jnp.exp2(s - top)
            exp_buf[pair, :, lanes] = e
            gp_buf[pair, :, lanes] = gp
            at = pl.ds(pair, 1)
            top_buf[at, lanes] = top
            sum_buf[at, lanes] = jnp.sum(e, axis=0, keepdims=True)
            dot_buf[at, lanes] = jnp.sum(e * gp, axis=0, keepdims=True)

    def second_half(pair, block, ds_at):
        grad_key = jnp.zeros((BLK, width), F32)
        grad_value = jnp.zeros((BLK, width), F32)
        for c in range(cuts):
            lanes = slice(c * chunk, (c + 1) * chunk)
            rows = slice(c * chunk, (c + 1) * chunk)
            at = pl.ds(pair, 1)
            a = exp_buf[pair, :, lanes] * fac_buf[at, lanes]
            ds = (a * (gp_buf[pair, :, lanes] - mean_buf[at, lanes])).astype(BF16)
            ds_buf[ds_at, lanes] = ds
            grad_value += jnp.dot(a.astype(BF16), go_buf[block, rows], preferred_element_type=F32)
            grad_key += jnp.dot(ds, q_buf[block, rows], preferred_element_type=F32)
        return grad_key * factor, grad_value

    def own_first(b):
        first_half(shards + b, b, kv_ref[0, at_block(b)], kv_ref[1, at_block(b)], True)

    load_q.wait()
    load_go.wait()
    own_first(0)

    @pl.loop(0, shards)
    def _(i):
        @pl.when(i > me)
        def _():
            ask_copy(i, i, i).wait_recv()
            asked = ask_in[i][0:1, :]
            total = jnp.zeros((2, BLK, width), F32)
            for q in range(blocks):
                hit = (asked == q).astype(F32)
                total = total + kv_ref[:, q * BLK : (q + 1) * BLK].astype(F32) * hit[None]
            kv_out[i] = total.astype(BF16)
            kv_copy(i, i, me).start()

    @pl.loop(1, blocks)
    def _(b):
        own_first(b)

    @pl.loop(0, shards)
    def _(i):
        @pl.when(i < me)
        def _():
            kv_copy(i, i, i).wait_recv()
            keys = slots[0, at_block(i)]
            for b in range(blocks):
                key_mask[b, at_block(i)] = (keys.astype(F32) * hit_ref[b, i]).astype(BF16)
            first_half(i, owner_ref[i], keys, slots[1, at_block(i)], False)

    fac = jnp.zeros((shards, rows_b), F32)
    mean = jnp.zeros((shards, rows_b), F32)
    for b in range(blocks):
        at = slice(shards + b, shards + b + 1)
        sel = sel_ref[b]
        far = top_buf[0:shards] + sel
        near = top_buf[at]
        top = jnp.maximum(jnp.max(far, axis=0, keepdims=True), near)
        far = jnp.exp2(far - top)
        near = jnp.exp2(near - top)
        inverse = 1.0 / (
            jnp.sum(far * sum_buf[0:shards], axis=0, keepdims=True) + near * sum_buf[at]
        )
        row_dot = inverse * (
            jnp.sum(far * dot_buf[0:shards], axis=0, keepdims=True) + near * dot_buf[at]
        )
        fac = fac + far * inverse
        mean = mean + jnp.where(sel == 0.0, 1.0, 0.0) * row_dot
        fac_buf[at] = near * inverse
        mean_buf[at] = row_dot
    fac_buf[0:shards] = fac
    mean_buf[0:shards] = mean

    @pl.loop(0, shards)
    def _(i):
        @pl.when(i < me)
        def _():
            grad_key, grad_value = second_half(i, owner_ref[i], at_block(i))
            ret_out[i, 0] = grad_key.astype(BF16)
            ret_out[i, 1] = grad_value.astype(BF16)
            ret_copy(i, i, me).start()

    @pl.loop(0, blocks)
    def _(b):
        grad_key, grad_value = second_half(shards + b, b, at_block(shards + b))
        own[0, at_block(b)] = grad_key
        own[1, at_block(b)] = grad_value
        far_t = key_mask[b].T
        near_t = kv_ref[0, at_block(b)].T
        for c in range(cuts):
            lanes = slice(c * chunk, (c + 1) * chunk)
            dq_t = jnp.dot(far_t, ds_buf[0 : shards * BLK, lanes], preferred_element_type=F32)
            dq_t += jnp.dot(near_t, ds_buf[at_block(shards + b), lanes], preferred_element_type=F32)
            dq_buf[b, lanes] = (dq_t * factor).T
        pltpu.make_async_copy(dq_buf.at[b], dq_hbm.at[b], dq_sem.at[b]).start()

    @pl.loop(0, shards)
    def _(i):
        @pl.when(i > me)
        def _():
            ret_copy(i, i, i).wait_recv()
            asked = ask_in[i][0:1, :]
            back = ret_in[i].astype(F32)
            for q in range(blocks):
                hit = (asked == q).astype(F32)
                own[:, q * BLK : (q + 1) * BLK] += back * hit[None]

    @pl.loop(0, peers)
    def _(i):
        @pl.when(i != mh)
        def _():
            hx_out[i] = own[:, pl.ds(pl.multiple_of(i * part, part), part)].astype(BF16)
            hx_copy(i, i, mh).start()

    hx_in[mh] = own[:, pl.ds(pl.multiple_of(mh * part, part), part)].astype(BF16)

    @pl.loop(0, peers)
    def _(i):
        @pl.when(i != mh)
        def _():
            hx_copy(i, i, i).wait_recv()

    for g in range(G):
        total = hx_in[g * run_total].astype(F32)
        for c in range(1, run_total):
            total = total + hx_in[g * run_total + c].astype(F32)
        out_ref[:, g] = total

    @pl.loop(0, shards)
    def _(i):
        @pl.when(i < me)
        def _():
            ask_copy(i, i, me).wait_send()
            ret_copy(i, i, me).wait_send()

        @pl.when(i > me)
        def _():
            kv_copy(i, i, me).wait_send()

    @pl.loop(0, peers)
    def _(i):
        @pl.when(i != mh)
        def _():
            hx_copy(i, i, mh).wait_send()

    @pl.loop(0, blocks)
    def _(b):
        pltpu.make_async_copy(dq_buf.at[b], dq_hbm.at[b], dq_sem.at[b]).wait()


def on_device(queries, key_states, values, grad_out, picked_blocks):
    tokens_dev, heads_dev, width = queries.shape
    blocks = tokens_dev // BLK
    shards = lax.axis_size("seq")
    peers = lax.axis_size("head")
    group_id = lax.axis_index("head") // (HPG // heads_dev)
    kv = jnp.stack([
        lax.dynamic_index_in_dim(key_states, group_id, 1, keepdims=False),
        lax.dynamic_index_in_dim(values, group_id, 1, keepdims=False),
    ])
    picks = lax.dynamic_index_in_dim(picked_blocks, group_id, 1, keepdims=False)[:, 1:]
    shard_ids = jnp.arange(shards, dtype=jnp.int32)
    match = (picks >= 0)[:, :, None] & ((picks // blocks)[:, :, None] == shard_ids)
    wanted = jnp.max(jnp.where(match, (picks % blocks)[:, :, None], -1), axis=(0, 1))
    hit = jnp.any(match, axis=1)
    block_ids = jnp.arange(blocks, dtype=jnp.int32)[:, None]
    owner = jnp.max(jnp.where(hit, block_ids, 0), axis=0)
    sel = jnp.where(hit, 0.0, NEG).astype(F32)[:, :, None]
    rows_b = tokens_dev * heads_dev // blocks
    chunk = min(512, rows_b)
    part = tokens_dev // peers
    pairs = shards + blocks
    dma = pltpu.SemaphoreType.DMA
    any_spec = pl.BlockSpec(memory_space=pl.ANY)
    vmem = pl.BlockSpec(memory_space=pltpu.VMEM)
    smem = pl.BlockSpec(memory_space=pltpu.SMEM)
    dq, out = pl.pallas_call(
        functools.partial(kernel, shards, peers, heads_dev, chunk),
        out_shape=(
            jax.ShapeDtypeStruct((blocks, rows_b, width), F32),
            jax.ShapeDtypeStruct((2, G, part, width), F32),
        ),
        in_specs=[any_spec, any_spec, vmem, smem, smem, smem, vmem],
        out_specs=(any_spec, vmem),
        scratch_shapes=[
            pltpu.VMEM((blocks, rows_b, width), BF16),
            pltpu.VMEM((blocks, rows_b, width), BF16),
            pltpu.VMEM((blocks, rows_b, width), F32),
            pltpu.VMEM((2, shards * BLK, width), BF16),
            pltpu.VMEM((blocks, shards * BLK, width), BF16),
            pltpu.VMEM((pairs, BLK, rows_b), F32),
            pltpu.VMEM((pairs, BLK, rows_b), F32),
            pltpu.VMEM((pairs * BLK, rows_b), BF16),
            pltpu.VMEM((pairs, rows_b), F32),
            pltpu.VMEM((pairs, rows_b), F32),
            pltpu.VMEM((pairs, rows_b), F32),
            pltpu.VMEM((pairs, rows_b), F32),
            pltpu.VMEM((pairs, rows_b), F32),
            pltpu.VMEM((2, tokens_dev, width), F32),
            pltpu.VMEM((shards, 8, 128), jnp.int32),
            pltpu.VMEM((shards, 8, 128), jnp.int32),
            pltpu.VMEM((shards, 2, BLK, width), BF16),
            pltpu.VMEM((shards, 2, BLK, width), BF16),
            pltpu.VMEM((shards, 2, BLK, width), BF16),
            pltpu.VMEM((peers, 2, part, width), BF16),
            pltpu.VMEM((peers, 2, part, width), BF16),
            dma((2,)), dma((blocks,)),
            dma((shards,)), dma((shards,)), dma((shards,)), dma((shards,)),
            dma((shards,)), dma((shards,)), dma((peers,)), dma((peers,)),
        ],
        compiler_params=pltpu.CompilerParams(
            collective_id=0, has_side_effects=True, vmem_limit_bytes=62 * 1024 * 1024
        ),
    )(
        queries.reshape(blocks, rows_b, width), grad_out.reshape(blocks, rows_b, width), kv,
        wanted, owner, hit.astype(F32), sel,
    )
    return (
        dq.reshape(tokens_dev, heads_dev, width),
        out[0].transpose(1, 0, 2),
        out[1].transpose(1, 0, 2),
    )


def solution(mesh):
    placed = (
        P("seq", "head", None),
        P("seq", None, None),
        P("seq", None, None),
        P("seq", "head", None),
        P("seq", None, None),
    )
    return jax.shard_map(
        on_device,
        mesh=mesh,
        in_specs=placed,
        out_specs=(
            P("seq", "head", None),
            P(("seq", "head"), None, None),
            P(("seq", "head"), None, None),
        ),
        check_vma=False,
    )
```

```python
import functools
import math

import jax
import jax.numpy as jnp
from jax import lax
from jax.experimental import pallas as pl
from jax.experimental.pallas import tpu as pltpu
from jax.sharding import PartitionSpec as P

G = 4
HPG = 16
BLK = 64
NEG = -1e30
FAR_UNROLL = 8
MESH = pl.DeviceIdType.MESH
F32 = jnp.float32
BF16 = jnp.bfloat16
NT = (((1,), (1,)), ((), ()))


def kernel(
    shards, peers, heads_dev, chunk,
    q_hbm, go_hbm, kv_ref, wanted_ref, owner_ref, hit_ref, sel_ref,
    dq_ref, out_ref,
    q_buf, go_buf, slots, key_mask, exp_buf, gp_buf, ds_buf,
    top_buf, sum_buf, dot_buf, fac_buf, mean_buf, own,
    ask_out, ask_in, kv_out, ret_out, ret_in, hx_out, hx_in,
    load_sem, ask_ssem, ask_rsem, kv_ssem, kv_rsem,
    ret_ssem, ret_rsem, hx_ssem, hx_rsem,
):
    me = lax.axis_index("seq")
    mh = lax.axis_index("head")
    width = q_hbm.shape[2]
    factor = width ** (-0.5)
    scale = factor * math.log2(math.e)
    blocks = kv_ref.shape[1] // BLK
    rows_b = q_buf.shape[1]
    part = kv_ref.shape[1] // peers
    run_total = HPG // heads_dev
    cuts = rows_b // chunk

    def at_block(i):
        return pl.ds(pl.multiple_of(i * BLK, BLK), BLK)

    def seq_copy(src, dst, ssem, rsem, peer):
        return pltpu.make_async_remote_copy(
            src_ref=src, dst_ref=dst, send_sem=ssem, recv_sem=rsem,
            device_id=(peer, mh), device_id_type=MESH,
        )

    def ask_copy(src_at, to, frm):
        return seq_copy(ask_out.at[src_at], ask_in.at[frm], ask_ssem.at[src_at], ask_rsem.at[frm], to)

    def kv_copy(src_at, to, frm):
        return seq_copy(
            kv_out.at[src_at], slots.at[:, at_block(frm)], kv_ssem.at[src_at], kv_rsem.at[frm], to
        )

    def ret_copy(src_at, to, frm):
        return seq_copy(ret_out.at[src_at], ret_in.at[frm], ret_ssem.at[src_at], ret_rsem.at[frm], to)

    def hx_copy(src_at, to, frm):
        return pltpu.make_async_remote_copy(
            src_ref=hx_out.at[src_at], dst_ref=hx_in.at[frm],
            send_sem=hx_ssem.at[src_at], recv_sem=hx_rsem.at[frm],
            device_id=(me, to), device_id_type=MESH,
        )

    load_q = pltpu.make_async_copy(q_hbm, q_buf, load_sem.at[0])
    load_go = pltpu.make_async_copy(go_hbm, go_buf, load_sem.at[1])
    load_q.start()
    load_go.start()

    barrier = pltpu.get_barrier_semaphore()

    @pl.loop(0, shards)
    def _(i):
        @pl.when(i != me)
        def _():
            pl.semaphore_signal(barrier, inc=1, device_id=(i, mh), device_id_type=MESH)

    @pl.loop(0, peers)
    def _(i):
        @pl.when(i != mh)
        def _():
            pl.semaphore_signal(barrier, inc=1, device_id=(me, i), device_id_type=MESH)

    @pl.loop(0, shards)
    def _(i):
        ask_out[i] = jnp.full((8, 128), wanted_ref[i], jnp.int32)

        @pl.when(i >= me)
        def _():
            slots[:, at_block(i)] = jnp.zeros((2, BLK, width), BF16)

    pl.semaphore_wait(barrier, shards + peers - 2)

    @pl.loop(0, shards)
    def _(i):
        @pl.when(i < me)
        def _():
            ask_copy(i, i, me).start()

    def first_half(pair, block, keys, vals, causal):
        for c in range(cuts):
            lanes = slice(c * chunk, (c + 1) * chunk)
            rows = slice(c * chunk, (c + 1) * chunk)
            s = lax.dot_general(keys, q_buf[block, rows], NT, preferred_element_type=F32) * scale
            if causal:
                key_row = lax.broadcasted_iota(jnp.int32, (BLK, chunk), 0)
                lane = lax.broadcasted_iota(jnp.int32, (BLK, chunk), 1)
                s = jnp.where(key_row * heads_dev <= lane + c * chunk, s, NEG)
            gp = lax.dot_general(vals, go_buf[block, rows], NT, preferred_element_type=F32)
            top = jnp.max(s, axis=0, keepdims=True)
            e = jnp.exp2(s - top)
            exp_buf[pair, :, lanes] = e
            gp_buf[pair, :, lanes] = gp
            at = pl.ds(pair, 1)
            top_buf[at, lanes] = top
            sum_buf[at, lanes] = jnp.sum(e, axis=0, keepdims=True)
            dot_buf[at, lanes] = jnp.sum(e * gp, axis=0, keepdims=True)

    def second_half(pair, block, ds_at):
        grad_key = jnp.zeros((BLK, width), F32)
        grad_value = jnp.zeros((BLK, width), F32)
        for c in range(cuts):
            lanes = slice(c * chunk, (c + 1) * chunk)
            rows = slice(c * chunk, (c + 1) * chunk)
            at = pl.ds(pair, 1)
            a = exp_buf[pair, :, lanes] * fac_buf[at, lanes]
            ds = (a * (gp_buf[pair, :, lanes] - mean_buf[at, lanes])).astype(BF16)
            ds_buf[ds_at, lanes] = ds
            grad_value += jnp.dot(a.astype(BF16), go_buf[block, rows], preferred_element_type=F32)
            grad_key += jnp.dot(ds, q_buf[block, rows], preferred_element_type=F32)
        return grad_key * factor, grad_value

    def own_first(b):
        first_half(shards + b, b, kv_ref[0, at_block(b)], kv_ref[1, at_block(b)], True)

    load_q.wait()
    load_go.wait()
    own_first(0)

    @pl.loop(0, shards)
    def _(i):
        @pl.when(i > me)
        def _():
            ask_copy(i, i, i).wait_recv()
            asked = ask_in[i][0:1, :]
            total = jnp.zeros((2, BLK, width), F32)
            for q in range(blocks):
                hit = (asked == q).astype(F32)
                total = total + kv_ref[:, q * BLK : (q + 1) * BLK].astype(F32) * hit[None]
            kv_out[i] = total.astype(BF16)
            kv_copy(i, i, me).start()

    for b in range(1, blocks):
        own_first(b)

    @pl.loop(0, shards)
    def _(i):
        @pl.when(i < me)
        def _():
            kv_copy(i, i, i).wait_recv()

    def each_far(body):
        if shards - 1 <= FAR_UNROLL:
            for i in range(shards - 1):
                body(i)
        else:
            pl.loop(0, shards - 1)(body)

    def far_first(i):
        keys = slots[0, at_block(i)]
        for b in range(blocks):
            key_mask[b, at_block(i)] = (keys.astype(F32) * hit_ref[b, i]).astype(BF16)
        first_half(i, owner_ref[i], keys, slots[1, at_block(i)], False)

    each_far(far_first)

    last = shards - 1
    top_buf[last : last + 1] = jnp.zeros((1, rows_b), F32)
    sum_buf[last : last + 1] = jnp.zeros((1, rows_b), F32)
    dot_buf[last : last + 1] = jnp.zeros((1, rows_b), F32)
    ds_buf[at_block(last)] = jnp.zeros((BLK, rows_b), BF16)
    for b in range(blocks):
        key_mask[b, at_block(last)] = jnp.zeros((BLK, width), BF16)

    fac = jnp.zeros((shards, rows_b), F32)
    mean = jnp.zeros((shards, rows_b), F32)
    for b in range(blocks):
        at = slice(shards + b, shards + b + 1)
        sel = sel_ref[b]
        far = top_buf[0:shards] + sel
        near = top_buf[at]
        top = jnp.maximum(jnp.max(far, axis=0, keepdims=True), near)
        far = jnp.exp2(far - top)
        near = jnp.exp2(near - top)
        inverse = 1.0 / (
            jnp.sum(far * sum_buf[0:shards], axis=0, keepdims=True) + near * sum_buf[at]
        )
        row_dot = inverse * (
            jnp.sum(far * dot_buf[0:shards], axis=0, keepdims=True) + near * dot_buf[at]
        )
        fac = fac + far * inverse
        mean = mean + jnp.where(sel == 0.0, 1.0, 0.0) * row_dot
        fac_buf[at] = near * inverse
        mean_buf[at] = row_dot
    fac_buf[0:shards] = fac
    mean_buf[0:shards] = mean

    def far_second(i):
        grad_key, grad_value = second_half(i, owner_ref[i], at_block(i))
        ret_out[i, 0] = grad_key.astype(BF16)
        ret_out[i, 1] = grad_value.astype(BF16)

    each_far(far_second)

    @pl.loop(0, shards)
    def _(i):
        @pl.when(i < me)
        def _():
            ret_copy(i, i, me).start()

    for b in range(blocks):
        grad_key, grad_value = second_half(shards + b, b, at_block(shards + b))
        own[0, at_block(b)] = grad_key
        own[1, at_block(b)] = grad_value
        far_t = key_mask[b].T
        near_t = kv_ref[0, at_block(b)].T
        for c in range(cuts):
            lanes = slice(c * chunk, (c + 1) * chunk)
            dq_t = jnp.dot(far_t, ds_buf[0 : shards * BLK, lanes], preferred_element_type=F32)
            dq_t += jnp.dot(near_t, ds_buf[at_block(shards + b), lanes], preferred_element_type=F32)
            dq_ref[b, lanes] = (dq_t * factor).T.astype(BF16)

    @pl.loop(0, shards)
    def _(i):
        @pl.when(i > me)
        def _():
            ret_copy(i, i, i).wait_recv()
            asked = ask_in[i][0:1, :]
            back = ret_in[i].astype(F32)
            for q in range(blocks):
                hit = (asked == q).astype(F32)
                own[:, q * BLK : (q + 1) * BLK] += back * hit[None]

    @pl.loop(0, peers)
    def _(i):
        @pl.when(i != mh)
        def _():
            hx_out[i] = own[:, pl.ds(pl.multiple_of(i * part, part), part)].astype(BF16)
            hx_copy(i, i, mh).start()

    hx_in[mh] = own[:, pl.ds(pl.multiple_of(mh * part, part), part)].astype(BF16)

    @pl.loop(0, peers)
    def _(i):
        @pl.when(i != mh)
        def _():
            hx_copy(i, i, i).wait_recv()

    for g in range(G):
        total = hx_in[g * run_total].astype(F32)
        for c in range(1, run_total):
            total = total + hx_in[g * run_total + c].astype(F32)
        out_ref[:, g] = total

    @pl.loop(0, shards)
    def _(i):
        @pl.when(i < me)
        def _():
            ask_copy(i, i, me).wait_send()
            ret_copy(i, i, me).wait_send()

        @pl.when(i > me)
        def _():
            kv_copy(i, i, me).wait_send()

    @pl.loop(0, peers)
    def _(i):
        @pl.when(i != mh)
        def _():
            hx_copy(i, i, mh).wait_send()


def on_device(queries, key_states, values, grad_out, picked_blocks):
    tokens_dev, heads_dev, width = queries.shape
    blocks = tokens_dev // BLK
    shards = lax.axis_size("seq")
    peers = lax.axis_size("head")
    group_id = lax.axis_index("head") // (HPG // heads_dev)
    kv = jnp.stack([
        lax.dynamic_index_in_dim(key_states, group_id, 1, keepdims=False),
        lax.dynamic_index_in_dim(values, group_id, 1, keepdims=False),
    ])
    picks = lax.dynamic_index_in_dim(picked_blocks, group_id, 1, keepdims=False)[:, 1:]
    shard_ids = jnp.arange(shards, dtype=jnp.int32)
    match = (picks >= 0)[:, :, None] & ((picks // blocks)[:, :, None] == shard_ids)
    wanted = jnp.max(jnp.where(match, (picks % blocks)[:, :, None], -1), axis=(0, 1))
    hit = jnp.any(match, axis=1)
    block_ids = jnp.arange(blocks, dtype=jnp.int32)[:, None]
    owner = jnp.max(jnp.where(hit, block_ids, 0), axis=0)
    sel = jnp.where(hit, 0.0, NEG).astype(F32)[:, :, None]
    rows_b = tokens_dev * heads_dev // blocks
    chunk = min(512, rows_b)
    part = tokens_dev // peers
    pairs = shards + blocks
    dma = pltpu.SemaphoreType.DMA
    hbm = pl.BlockSpec(memory_space=pltpu.HBM)
    vmem = pl.BlockSpec(memory_space=pltpu.VMEM)
    smem = pl.BlockSpec(memory_space=pltpu.SMEM)
    dq, out = pl.pallas_call(
        functools.partial(kernel, shards, peers, heads_dev, chunk),
        out_shape=(
            jax.ShapeDtypeStruct((blocks, rows_b, width), BF16),
            jax.ShapeDtypeStruct((2, G, part, width), F32),
        ),
        in_specs=[hbm, hbm, vmem, smem, smem, smem, vmem],
        out_specs=(vmem, vmem),
        scratch_shapes=[
            pltpu.VMEM((blocks, rows_b, width), BF16),
            pltpu.VMEM((blocks, rows_b, width), BF16),
            pltpu.VMEM((2, shards * BLK, width), BF16),
            pltpu.VMEM((blocks, shards * BLK, width), BF16),
            pltpu.VMEM((pairs, BLK, rows_b), F32),
            pltpu.VMEM((pairs, BLK, rows_b), F32),
            pltpu.VMEM((pairs * BLK, rows_b), BF16),
            pltpu.VMEM((pairs, rows_b), F32),
            pltpu.VMEM((pairs, rows_b), F32),
            pltpu.VMEM((pairs, rows_b), F32),
            pltpu.VMEM((pairs, rows_b), F32),
            pltpu.VMEM((pairs, rows_b), F32),
            pltpu.VMEM((2, tokens_dev, width), F32),
            pltpu.VMEM((shards, 8, 128), jnp.int32),
            pltpu.VMEM((shards, 8, 128), jnp.int32),
            pltpu.VMEM((shards, 2, BLK, width), BF16),
            pltpu.VMEM((shards, 2, BLK, width), BF16),
            pltpu.VMEM((shards, 2, BLK, width), BF16),
            pltpu.VMEM((peers, 2, part, width), BF16),
            pltpu.VMEM((peers, 2, part, width), BF16),
            dma((2,)),
            dma((shards,)), dma((shards,)), dma((shards,)), dma((shards,)),
            dma((shards,)), dma((shards,)), dma((peers,)), dma((peers,)),
        ],
        compiler_params=pltpu.CompilerParams(
            collective_id=0, has_side_effects=True, vmem_limit_bytes=52 * 1024 * 1024
        ),
    )(
        queries.reshape(blocks, rows_b, width), grad_out.reshape(blocks, rows_b, width), kv,
        wanted, owner, hit.astype(F32), sel,
    )
    return (
        dq.reshape(tokens_dev, heads_dev, width).astype(F32),
        out[0].transpose(1, 0, 2),
        out[1].transpose(1, 0, 2),
    )


def solution(mesh):
    placed = (
        P("seq", "head", None),
        P("seq", None, None),
        P("seq", None, None),
        P("seq", "head", None),
        P("seq", None, None),
    )
    return jax.shard_map(
        on_device,
        mesh=mesh,
        in_specs=placed,
        out_specs=(
            P("seq", "head", None),
            P(("seq", "head"), None, None),
            P(("seq", "head"), None, None),
        ),
        check_vma=False,
    )
```

```python
import functools
import math

import jax
import jax.numpy as jnp
from jax import lax
from jax.experimental import pallas as pl
from jax.experimental.pallas import tpu as pltpu
from jax.sharding import PartitionSpec as P

G = 4
HPG = 16
BLK = 64
NEG = -1e30
FAR_UNROLL = 8
MESH = pl.DeviceIdType.MESH
F32 = jnp.float32
BF16 = jnp.bfloat16
NT = (((1,), (1,)), ((), ()))


def kernel(
    shards, peers, heads_dev, chunk,
    q_hbm, go_hbm, kv_ref, wanted_ref, owner_ref, hit_ref, sel_ref,
    dq_ref, out_ref,
    q_buf, go_buf, slots, key_mask, exp_buf, gp_buf, ds_buf,
    top_buf, sum_buf, dot_buf, fac_buf, mean_buf, own,
    ask_out, ask_in, kv_out, ret_out, ret_in, hx_out, hx_in,
    load_sem, ask_ssem, ask_rsem, kv_ssem, kv_rsem,
    ret_ssem, ret_rsem, hx_ssem, hx_rsem,
):
    me = lax.axis_index("seq")
    mh = lax.axis_index("head")
    width = q_hbm.shape[2]
    factor = width ** (-0.5)
    scale = factor * math.log2(math.e)
    blocks = kv_ref.shape[1] // BLK
    rows_b = q_buf.shape[1]
    part = kv_ref.shape[1] // peers
    run_total = HPG // heads_dev
    cuts = rows_b // chunk

    def at_block(i):
        return pl.ds(pl.multiple_of(i * BLK, BLK), BLK)

    def seq_copy(src, dst, ssem, rsem, peer):
        return pltpu.make_async_remote_copy(
            src_ref=src, dst_ref=dst, send_sem=ssem, recv_sem=rsem,
            device_id=(peer, mh), device_id_type=MESH,
        )

    def ask_copy(src_at, to, frm):
        return seq_copy(ask_out.at[src_at], ask_in.at[frm], ask_ssem.at[src_at], ask_rsem.at[frm], to)

    def kv_copy(src_at, to, frm):
        return seq_copy(
            kv_out.at[src_at], slots.at[:, at_block(frm)], kv_ssem.at[src_at], kv_rsem.at[frm], to
        )

    def ret_copy(src_at, to, frm):
        return seq_copy(ret_out.at[src_at], ret_in.at[frm], ret_ssem.at[src_at], ret_rsem.at[frm], to)

    def hx_copy(src_at, to, frm):
        return pltpu.make_async_remote_copy(
            src_ref=hx_out.at[src_at], dst_ref=hx_in.at[frm],
            send_sem=hx_ssem.at[src_at], recv_sem=hx_rsem.at[frm],
            device_id=(me, to), device_id_type=MESH,
        )

    load_q = pltpu.make_async_copy(q_hbm, q_buf, load_sem.at[0])
    load_go = pltpu.make_async_copy(go_hbm, go_buf, load_sem.at[1])
    load_q.start()
    load_go.start()

    barrier = pltpu.get_barrier_semaphore()

    @pl.loop(0, shards)
    def _(i):
        @pl.when(i != me)
        def _():
            pl.semaphore_signal(barrier, inc=1, device_id=(i, mh), device_id_type=MESH)

    @pl.loop(0, peers)
    def _(i):
        @pl.when(i != mh)
        def _():
            pl.semaphore_signal(barrier, inc=1, device_id=(me, i), device_id_type=MESH)

    @pl.loop(0, shards)
    def _(i):
        ask_out[i] = jnp.full((8, 128), wanted_ref[i], jnp.int32)

        @pl.when(i >= me)
        def _():
            slots[:, at_block(i)] = jnp.zeros((2, BLK, width), BF16)

    pl.semaphore_wait(barrier, shards + peers - 2)

    @pl.loop(0, shards)
    def _(i):
        @pl.when(i < me)
        def _():
            ask_copy(i, i, me).start()

    def first_half(pair, block, keys, vals, causal):
        for c in range(cuts):
            lanes = slice(c * chunk, (c + 1) * chunk)
            rows = slice(c * chunk, (c + 1) * chunk)
            s = lax.dot_general(keys, q_buf[block, rows], NT, preferred_element_type=F32) * scale
            if causal:
                key_row = lax.broadcasted_iota(jnp.int32, (BLK, chunk), 0)
                lane = lax.broadcasted_iota(jnp.int32, (BLK, chunk), 1)
                s = jnp.where(key_row * heads_dev <= lane + c * chunk, s, NEG)
            gp = lax.dot_general(vals, go_buf[block, rows], NT, preferred_element_type=F32)
            top = jnp.max(s, axis=0, keepdims=True)
            e = jnp.exp2(s - top)
            exp_buf[pair, :, lanes] = e
            gp_buf[pair, :, lanes] = gp
            at = pl.ds(pair, 1)
            top_buf[at, lanes] = top
            sum_buf[at, lanes] = jnp.sum(e, axis=0, keepdims=True)
            dot_buf[at, lanes] = jnp.sum(e * gp, axis=0, keepdims=True)

    def second_half(pair, block, ds_at):
        grad_key = jnp.zeros((BLK, width), F32)
        grad_value = jnp.zeros((BLK, width), F32)
        for c in range(cuts):
            lanes = slice(c * chunk, (c + 1) * chunk)
            rows = slice(c * chunk, (c + 1) * chunk)
            at = pl.ds(pair, 1)
            a = exp_buf[pair, :, lanes] * fac_buf[at, lanes]
            ds = (a * (gp_buf[pair, :, lanes] - mean_buf[at, lanes])).astype(BF16)
            ds_buf[ds_at, lanes] = ds
            grad_value += jnp.dot(a.astype(BF16), go_buf[block, rows], preferred_element_type=F32)
            grad_key += jnp.dot(ds, q_buf[block, rows], preferred_element_type=F32)
        return grad_key * factor, grad_value

    def own_first(b):
        first_half(shards + b, b, kv_ref[0, at_block(b)], kv_ref[1, at_block(b)], True)

    load_q.wait()
    load_go.wait()
    own_first(0)

    @pl.loop(0, shards)
    def _(i):
        @pl.when(i > me)
        def _():
            ask_copy(i, i, i).wait_recv()
            asked = ask_in[i][0:1, :]
            total = jnp.zeros((2, BLK, width), F32)
            for q in range(blocks):
                hit = (asked == q).astype(F32)
                total = total + kv_ref[:, q * BLK : (q + 1) * BLK].astype(F32) * hit[None]
            kv_out[i] = total.astype(BF16)
            kv_copy(i, i, me).start()

    for b in range(1, blocks):
        own_first(b)

    @pl.loop(0, shards)
    def _(i):
        @pl.when(i < me)
        def _():
            kv_copy(i, i, i).wait_recv()

    def each_far(body):
        if shards - 1 <= FAR_UNROLL:
            for i in range(shards - 1):
                body(i)
        else:
            pl.loop(0, shards - 1)(body)

    def far_first(i):
        keys = slots[0, at_block(i)]
        for b in range(blocks):
            key_mask[b, at_block(i)] = (keys.astype(F32) * hit_ref[b, i]).astype(BF16)
        first_half(i, owner_ref[i], keys, slots[1, at_block(i)], False)

    each_far(far_first)

    last = shards - 1
    top_buf[last : last + 1] = jnp.zeros((1, rows_b), F32)
    sum_buf[last : last + 1] = jnp.zeros((1, rows_b), F32)
    dot_buf[last : last + 1] = jnp.zeros((1, rows_b), F32)
    ds_buf[at_block(last)] = jnp.zeros((BLK, rows_b), BF16)
    for b in range(blocks):
        key_mask[b, at_block(last)] = jnp.zeros((BLK, width), BF16)

    fac = jnp.zeros((shards, rows_b), F32)
    mean = jnp.zeros((shards, rows_b), F32)
    for b in range(blocks):
        at = slice(shards + b, shards + b + 1)
        sel = sel_ref[b]
        far = top_buf[0:shards] + sel
        near = top_buf[at]
        top = jnp.maximum(jnp.max(far, axis=0, keepdims=True), near)
        far = jnp.exp2(far - top)
        near = jnp.exp2(near - top)
        inverse = 1.0 / (
            jnp.sum(far * sum_buf[0:shards], axis=0, keepdims=True) + near * sum_buf[at]
        )
        row_dot = inverse * (
            jnp.sum(far * dot_buf[0:shards], axis=0, keepdims=True) + near * dot_buf[at]
        )
        fac = fac + far * inverse
        mean = mean + jnp.where(sel == 0.0, 1.0, 0.0) * row_dot
        fac_buf[at] = near * inverse
        mean_buf[at] = row_dot
    fac_buf[0:shards] = fac
    mean_buf[0:shards] = mean

    def far_second(i):
        grad_key, grad_value = second_half(i, owner_ref[i], at_block(i))
        ret_out[i, 0] = grad_key.astype(BF16)
        ret_out[i, 1] = grad_value.astype(BF16)

    def send_back(i):
        @pl.when(i < me)
        def _():
            ret_copy(i, i, me).start()

    if shards - 1 <= FAR_UNROLL:
        for start in range(0, shards - 1, 2):
            group = range(start, min(start + 2, shards - 1))
            for i in group:
                far_second(i)
            for i in group:
                send_back(i)
    else:

        @pl.loop(0, shards - 1)
        def _(i):
            far_second(i)
            send_back(i)

    for b in range(blocks):
        grad_key, grad_value = second_half(shards + b, b, at_block(shards + b))
        own[0, at_block(b)] = grad_key
        own[1, at_block(b)] = grad_value
        far_t = key_mask[b].T
        near_t = kv_ref[0, at_block(b)].T
        for c in range(cuts):
            lanes = slice(c * chunk, (c + 1) * chunk)
            dq_t = jnp.dot(far_t, ds_buf[0 : shards * BLK, lanes], preferred_element_type=F32)
            dq_t += jnp.dot(near_t, ds_buf[at_block(shards + b), lanes], preferred_element_type=F32)
            dq_ref[b, lanes] = (dq_t * factor).T.astype(BF16)

    @pl.loop(0, shards)
    def _(i):
        @pl.when(i > me)
        def _():
            ret_copy(i, i, i).wait_recv()
            asked = ask_in[i][0:1, :]
            back = ret_in[i].astype(F32)
            for q in range(blocks):
                hit = (asked == q).astype(F32)
                own[:, q * BLK : (q + 1) * BLK] += back * hit[None]

    @pl.loop(0, peers)
    def _(i):
        @pl.when(i != mh)
        def _():
            hx_out[i] = own[:, pl.ds(pl.multiple_of(i * part, part), part)].astype(BF16)
            hx_copy(i, i, mh).start()

    hx_in[mh] = own[:, pl.ds(pl.multiple_of(mh * part, part), part)].astype(BF16)

    @pl.loop(0, peers)
    def _(i):
        @pl.when(i != mh)
        def _():
            hx_copy(i, i, i).wait_recv()

    for g in range(G):
        total = hx_in[g * run_total].astype(F32)
        for c in range(1, run_total):
            total = total + hx_in[g * run_total + c].astype(F32)
        for t in range(2):
            out_ref[t, :, g, :] = total[t]

    @pl.loop(0, shards)
    def _(i):
        @pl.when(i < me)
        def _():
            ask_copy(i, i, me).wait_send()
            ret_copy(i, i, me).wait_send()

        @pl.when(i > me)
        def _():
            kv_copy(i, i, me).wait_send()

    @pl.loop(0, peers)
    def _(i):
        @pl.when(i != mh)
        def _():
            hx_copy(i, i, mh).wait_send()


def on_device(queries, key_states, values, grad_out, picked_blocks):
    tokens_dev, heads_dev, width = queries.shape
    blocks = tokens_dev // BLK
    shards = lax.axis_size("seq")
    peers = lax.axis_size("head")
    group_id = lax.axis_index("head") // (HPG // heads_dev)
    kv = jnp.stack([
        lax.dynamic_index_in_dim(key_states, group_id, 1, keepdims=False),
        lax.dynamic_index_in_dim(values, group_id, 1, keepdims=False),
    ])
    picks = lax.dynamic_index_in_dim(picked_blocks, group_id, 1, keepdims=False)[:, 1:]
    shard_ids = jnp.arange(shards, dtype=jnp.int32)
    match = (picks >= 0)[:, :, None] & ((picks // blocks)[:, :, None] == shard_ids)
    wanted = jnp.max(jnp.where(match, (picks % blocks)[:, :, None], -1), axis=(0, 1))
    hit = jnp.any(match, axis=1)
    block_ids = jnp.arange(blocks, dtype=jnp.int32)[:, None]
    owner = jnp.max(jnp.where(hit, block_ids, 0), axis=0)
    sel = jnp.where(hit, 0.0, NEG).astype(F32)[:, :, None]
    rows_b = tokens_dev * heads_dev // blocks
    chunk = min(512, rows_b)
    part = tokens_dev // peers
    pairs = shards + blocks
    dma = pltpu.SemaphoreType.DMA
    hbm = pl.BlockSpec(memory_space=pltpu.HBM)
    vmem = pl.BlockSpec(memory_space=pltpu.VMEM)
    smem = pl.BlockSpec(memory_space=pltpu.SMEM)
    dq, out = pl.pallas_call(
        functools.partial(kernel, shards, peers, heads_dev, chunk),
        out_shape=(
            jax.ShapeDtypeStruct((blocks, rows_b, width), BF16),
            jax.ShapeDtypeStruct((2, part, G, width), F32),
        ),
        in_specs=[hbm, hbm, vmem, smem, smem, smem, vmem],
        out_specs=(vmem, vmem),
        scratch_shapes=[
            pltpu.VMEM((blocks, rows_b, width), BF16),
            pltpu.VMEM((blocks, rows_b, width), BF16),
            pltpu.VMEM((2, shards * BLK, width), BF16),
            pltpu.VMEM((blocks, shards * BLK, width), BF16),
            pltpu.VMEM((pairs, BLK, rows_b), F32),
            pltpu.VMEM((pairs, BLK, rows_b), F32),
            pltpu.VMEM((pairs * BLK, rows_b), BF16),
            pltpu.VMEM((pairs, rows_b), F32),
            pltpu.VMEM((pairs, rows_b), F32),
            pltpu.VMEM((pairs, rows_b), F32),
            pltpu.VMEM((pairs, rows_b), F32),
            pltpu.VMEM((pairs, rows_b), F32),
            pltpu.VMEM((2, tokens_dev, width), F32),
            pltpu.VMEM((shards, 8, 128), jnp.int32),
            pltpu.VMEM((shards, 8, 128), jnp.int32),
            pltpu.VMEM((shards, 2, BLK, width), BF16),
            pltpu.VMEM((shards, 2, BLK, width), BF16),
            pltpu.VMEM((shards, 2, BLK, width), BF16),
            pltpu.VMEM((peers, 2, part, width), BF16),
            pltpu.VMEM((peers, 2, part, width), BF16),
            dma((2,)),
            dma((shards,)), dma((shards,)), dma((shards,)), dma((shards,)),
            dma((shards,)), dma((shards,)), dma((peers,)), dma((peers,)),
        ],
        compiler_params=pltpu.CompilerParams(
            collective_id=0, has_side_effects=True, vmem_limit_bytes=52 * 1024 * 1024
        ),
    )(
        queries.reshape(blocks, rows_b, width), grad_out.reshape(blocks, rows_b, width), kv,
        wanted, owner, hit.astype(F32), sel,
    )
    return (
        dq.reshape(tokens_dev, heads_dev, width).astype(F32),
        out[0],
        out[1],
    )


def solution(mesh):
    placed = (
        P("seq", "head", None),
        P("seq", None, None),
        P("seq", None, None),
        P("seq", "head", None),
        P("seq", None, None),
    )
    return jax.shard_map(
        on_device,
        mesh=mesh,
        in_specs=placed,
        out_specs=(
            P("seq", "head", None),
            P(("seq", "head"), None, None),
            P(("seq", "head"), None, None),
        ),
        check_vma=False,
    )
```
